32 devices in a mesh: slab: 4 (over y, x), tile: 8 (over z, core).
Axes of the slice: x: 2, y: 2, z: 4, core: 2. Of those that a mesh axis runs over, the one named last changes fastest.
Arguments:
- particles: float32 [7, 8, 16, 1536], P(None, 'slab', 'tile')
- counts: int32 [8, 16, 48], P('slab', 'tile'), may hold values from 10 to 32, as said below
- leavers: int32 [2, 4, 16, 48], P(None, 'slab', 'tile'), may hold values from 0 to 4, as said below
Outputs:
- kept: float32 [7, 8, 16, 1536], P(None, 'slab', 'tile')
- arrivals: float32 [2, 7, 6144], P(None, None, ('slab', 'tile'))
The draws below stay inside these ranges and needn't reach their ends.
Inputs may be any that keep to these rules, and one draw needn't show every extreme that they name: `counts`: one cell holds exactly 32. Over the 2 x 48 cells of one face of one device the leavers sum to exactly 192; one face cell of each face has 4.
All inputs are finite; a program needn't handle non-finite values.
Results may differ from the reference program's by a relative error of at most 0.0003.
Values sent between devices are 32-bit elements; how exact they have to be, the bound alone decides.
A program may use at most 128 MiB of HBM per device.

```python
import math
import jax
import jax.numpy as jnp
from jax import lax

CX = 2
CY = 2
CZ = 48
SLOTS = 32
LMAX = 4
SLABS = 4
TILES = 8
NX = 8
NY = 16
FACE_ROWS = 192


def draw_particles(key, part):
    subkeys = jax.random.split(jax.random.fold_in(key, 11), 3)
    grid_shape = (NX, NY, CZ * SLOTS)
    position = jax.random.uniform(subkeys[0], (3,) + grid_shape, jnp.float32)
    velocity = 0.3 * jnp.clip(jax.random.normal(subkeys[1], (3,) + grid_shape, jnp.float32), -4.0, 4.0)
    density = 1.0 + 0.01 * jnp.clip(jax.random.normal(subkeys[2], (1,) + grid_shape, jnp.float32), -4.0, 4.0)
    return jnp.concatenate([position, velocity, density], axis=0)


def draw_counts(key, part):
    subkeys = jax.random.split(jax.random.fold_in(key, 23), 3)
    grid_shape = (NX, NY, CZ)
    front_x = jax.random.randint(subkeys[0], (), 0, NX - 1)
    column = lax.broadcasted_iota(jnp.int32, grid_shape, 0)
    across = lax.broadcasted_iota(jnp.int32, grid_shape, 1)
    upward = lax.broadcasted_iota(jnp.int32, grid_shape, 2)
    band = (column == front_x) | (column == front_x + 1)
    dense = jax.random.randint(subkeys[1], grid_shape, SLOTS - 4, SLOTS + 1)
    sparse = jax.random.randint(subkeys[2], grid_shape, 5 * SLOTS // 16, 5 * SLOTS // 8 + 1)
    filled = jnp.where(band, dense, sparse)
    anchor = (column == front_x) & (across == 0) & (upward == 0)
    return jnp.where(anchor, SLOTS, filled).astype(jnp.int32)


def draw_leavers(key, part):
    tile_count = NY // CY
    block_count = 2 * SLABS * tile_count
    cell_total = CY * CZ
    pair_total = cell_total // 2
    block_keys = jax.random.split(jax.random.fold_in(key, 37), block_count)

    def one_face(block_key):
        order_key, spread_key = jax.random.split(block_key)
        order = jax.random.permutation(order_key, cell_total)
        spread = jax.random.randint(spread_key, (pair_total,), 0, LMAX // 2 + 1)
        spread = spread.at[0].set(LMAX // 2)
        values = jnp.concatenate([LMAX // 2 + spread, LMAX // 2 - spread]).astype(jnp.int32)
        return jnp.zeros((cell_total,), jnp.int32).at[order].set(values)
    faces = jax.vmap(one_face)(block_keys)
    return faces.reshape(2, SLABS, NY, CZ)


def setup_inputs(seed: int = 0) -> dict:
    key_list = jax.random.split(jax.random.key(seed), 4)
    particles = draw_particles(jax.random.fold_in(key_list[3], 71), 0)
    counts = draw_counts(jax.random.fold_in(key_list[3], 71), 0)
    leavers = draw_leavers(jax.random.fold_in(key_list[3], 71), 0)
    return dict(particles=particles, counts=counts, leavers=leavers)


sound_speed = 10.0
smoothing = 0.5
cell_side = 2.0 * smoothing
kernel_norm = 21.0 / (16.0 * math.pi * smoothing ** 3)
grad_scale = -5.0 * kernel_norm / (smoothing * smoothing)
eos_stiff = sound_speed * sound_speed / 7.0
particle_mass = 0.125
viscosity = 0.1
visc_floor = 0.01 * smoothing * smoothing
time_step = 0.01
gravity = 9.81
layer_block = 4

def occupied(cell_counts):
    filled = jnp.repeat(cell_counts, SLOTS, axis=-1)
    slot_index = jnp.arange(filled.shape[-1], dtype=jnp.int32) % SLOTS
    return (slot_index < filled).astype(jnp.float32)

def pair_rates(center, beside_all):
    span_x, span_y, span_z = (center.shape[1], center.shape[2], center.shape[3])
    dens_c = center[6] + 1.0 - center[7]
    dens_n = beside_all[6] + 1.0 - beside_all[7]
    ratio_c = eos_stiff * (dens_c ** 7 - 1.0) / (dens_c * dens_c)
    ratio_n = eos_stiff * (dens_n ** 7 - 1.0) / (dens_n * dens_n)
    accel_sum = jnp.zeros((3,) + center.shape[1:], jnp.float32)
    drift_sum = jnp.zeros(center.shape[1:], jnp.float32)
    for step_x in range(3):
        for step_y in range(3):
            for step_z in range(3):
                neighbour = beside_all[:, step_x:step_x + span_x, step_y:step_y + span_y, step_z:step_z + span_z]
                near_dens = dens_n[step_x:step_x + span_x, step_y:step_y + span_y, step_z:step_z + span_z]
                near_ratio = ratio_n[step_x:step_x + span_x, step_y:step_y + span_y, step_z:step_z + span_z]
                cell_gap = jnp.array([float(1 - step_x), float(1 - step_y), float(1 - step_z)], jnp.float32).reshape(3, 1, 1, 1, 1, 1) * cell_side
                offset_vec = center[0:3, ..., None] - neighbour[0:3, ..., None, :] + cell_gap
                dist_sq = lax.optimization_barrier(jnp.sum(offset_vec * offset_vec, axis=0))
                support = jnp.maximum(1.0 - jnp.sqrt(dist_sq) / (2.0 * smoothing), 0.0)
                slope_term = grad_scale * support * support * support * neighbour[7][..., None, :]
                approach = lax.optimization_barrier(jnp.sum((center[3:6, ..., None] - neighbour[3:6, ..., None, :]) * offset_vec, axis=0))
                mean_dens = 0.5 * (dens_c[..., None] + near_dens[..., None, :])
                visc_term = -viscosity * sound_speed * smoothing * jnp.minimum(approach, 0.0) / ((dist_sq + visc_floor) * mean_dens)
                force_term = (ratio_c[..., None] + near_ratio[..., None, :] + visc_term) * slope_term
                accel_sum = accel_sum - particle_mass * lax.optimization_barrier(jnp.sum(force_term * offset_vec, axis=-1))
                drift_sum = drift_sum + particle_mass * lax.optimization_barrier(jnp.sum(slope_term * approach, axis=-1))
    gravity_vec = jnp.array([0.0, 0.0, gravity], jnp.float32).reshape(3, 1, 1, 1, 1)
    return jnp.concatenate([accel_sum - gravity_vec, drift_sum[None]], axis=0)

def region_rates(extended):
    span_x = extended.shape[1] - 2
    span_y = extended.shape[2] - 2
    layers = extended.shape[3] // SLOTS
    cells_grid = extended.reshape(8, span_x + 2, span_y + 2, layers, SLOTS)
    padded = jnp.pad(cells_grid, ((0, 0), (0, 0), (0, 0), (1, 1), (0, 0)))

    def one_block(block_index):
        layer_start = (block_index * layer_block).astype(jnp.int32)
        beside_all = lax.dynamic_slice_in_dim(padded, layer_start, layer_block + 2, axis=3)
        return pair_rates(beside_all[:, 1:-1, 1:-1, 1:-1], beside_all)
    stacked = lax.map(one_block, jnp.arange(layers // layer_block, dtype=jnp.int32))
    ordered = jnp.moveaxis(stacked, 0, 3)
    return ordered.reshape(4, span_x, span_y, layers * SLOTS)

def predict(fields, rates_now):
    position = fields[0:3] + 0.5 * time_step * fields[3:6]
    velocity = fields[3:6] + 0.5 * time_step * rates_now[0:3]
    density = fields[6:7] + 0.5 * time_step * rates_now[3:4]
    return jnp.concatenate([position, velocity, density, fields[7:8]], axis=0)

def correct(fields, rates_mid):
    velocity = fields[3:6] + time_step * rates_mid[0:3]
    density = fields[6:7] + time_step * rates_mid[3:4]
    position = fields[0:3] + 0.5 * time_step * (fields[3:6] + velocity)
    return jnp.concatenate([position, velocity, density], axis=0)

def pack_leavers(face_state, face_count, face_leave):
    cell_total = face_count.shape[0] * face_count.shape[1]
    row_total = cell_total * LMAX // 2
    leave_quota = face_leave.reshape(cell_total)
    occupancy = face_count.reshape(cell_total)
    row_ends = jnp.cumsum(leave_quota, dtype=jnp.int32)
    starts = row_ends - leave_quota
    row_ids = jnp.arange(row_total, dtype=jnp.int32)
    owner_mask = (starts[None, :] <= row_ids[:, None]) & (row_ends[None, :] > row_ids[:, None])
    root = jnp.arange(cell_total, dtype=jnp.int32) * SLOTS + occupancy - leave_quota - starts
    source_row = lax.optimization_barrier(jnp.sum(jnp.where(owner_mask, root[None, :], 0), axis=1, dtype=jnp.int32)) + row_ids
    flat_face = face_state.reshape(7, cell_total * SLOTS)
    return jnp.take(flat_face, source_row, axis=1)

def column_rates(extended, size_x):

    def one_column(column):
        strip = lax.dynamic_slice_in_dim(extended, column, 3, axis=1)
        return region_rates(strip)[:, 0]
    stacked = lax.map(one_column, jnp.arange(size_x, dtype=jnp.int32))
    return jnp.moveaxis(stacked, 0, 1)

def reference(particles, counts, leavers):
    size_x = particles.shape[1]
    fields = jnp.concatenate([particles, occupied(counts)[None]], axis=0)
    pad_plan = ((0, 0), (1, 1), (1, 1), (0, 0))
    rates_now = column_rates(jnp.pad(fields, pad_plan), size_x)
    midpoint = predict(fields, rates_now)
    updated = correct(fields, column_rates(jnp.pad(midpoint, pad_plan), size_x))
    grouped = counts.reshape(SLABS, CX, NY, CZ)
    grouped = grouped.at[:, 0].add(-leavers[0]).at[:, CX - 1].add(-leavers[1])
    kept = updated * occupied(grouped.reshape(NX, NY, CZ))[None]
    faces = updated.reshape(7, SLABS, CX, TILES, CY, CZ * SLOTS)
    face_counts = counts.reshape(SLABS, CX, TILES, CY, CZ)
    face_leave = leavers.reshape(2, SLABS, TILES, CY, CZ)
    packer = jax.vmap(jax.vmap(pack_leavers, in_axes=(1, 0, 0)), in_axes=(1, 0, 0))
    lower_rows = packer(faces[:, :, 0], face_counts[:, 0], face_leave[0])
    upper_rows = packer(faces[:, :, CX - 1], face_counts[:, CX - 1], face_leave[1])
    nothing = jnp.zeros_like(lower_rows[:1])
    from_below = jnp.concatenate([nothing, upper_rows[:-1]], axis=0)
    from_above = jnp.concatenate([lower_rows[1:], nothing], axis=0)
    arrivals = jnp.stack([from_below, from_above], axis=0)
    arrivals = jnp.transpose(arrivals, (0, 3, 1, 2, 4)).reshape(2, 7, SLABS * TILES * FACE_ROWS)
    return (kept, arrivals)
```

```python
import math

import jax
import jax.numpy as jnp
from jax import lax
from jax.experimental import pallas as pl
from jax.experimental.pallas import tpu as pltpu
from jax.sharding import PartitionSpec as P

SLOTS = 32
LMAX = 4

sound_speed = 10.0
smoothing = 0.5
kernel_norm = 21.0 / (16.0 * math.pi * smoothing**3)
grad_scale = -5.0 * kernel_norm / (smoothing * smoothing)
eos_stiff = sound_speed * sound_speed / 7.0
particle_mass = 0.125
viscosity = 0.1
visc_floor = 0.01 * smoothing * smoothing
time_step = 0.01
gravity = 9.81
visc_scale = 2.0 * viscosity * sound_speed * smoothing
far = 1.0e6
HALF = 16


def shifted(value, axis, steps):
    count = lax.axis_size(axis)
    leading, last = (max(0, -steps), min(count, count - steps))
    return lax.ppermute(value, axis, [(source, source + steps) for source in range(leading, last)])


def occupied(cell_counts):
    filled = jnp.repeat(cell_counts, SLOTS, axis=-1)
    slot_index = jnp.arange(filled.shape[-1], dtype=jnp.int32) % SLOTS
    return slot_index < filled


def packed_blocks(chunks, cy, lane, row):
    hole_group = 3 if cy == 0 else 0
    hole = (lane >= 32 * hole_group) & (lane < 32 * hole_group + 32)
    groups = (0, 1, 2) if cy == 0 else (1, 2, 3)
    blocks = []
    for n in range(6):
        group = groups[n % 3]
        moved = pltpu.roll(chunks[7 + n // 3], (32 * (hole_group - group)) % 128, 1)
        blocks.append(jnp.where(hole, moved, chunks[n]))
    blocks.append(jnp.where(hole & (row == 0), far, chunks[6]))
    return blocks


def level_rates(load, res_ref, pack_ref):
    lane = lax.broadcasted_iota(jnp.int32, (8, 128), 1)
    row = lax.broadcasted_iota(jnp.int32, (8, 128), 0)
    lane_half = lax.broadcasted_iota(jnp.int32, (HALF, 128), 1)
    for cx in range(2):
        chunks = [load(dz, cx + dx) for dz in range(3) for dx in range(3)]
        columns = jnp.transpose(load(1, cx + 1))
        for cy in range(2):
            cell = 2 * cx + cy
            blocks = packed_blocks(chunks, cy, lane, row)
            for n in range(7):
                pack_ref[cell, n] = blocks[n]
            for half in range(SLOTS // HALF):
                first = 32 * (cy + 1) + HALF * half
                own = [
                    jnp.broadcast_to(columns[first : first + HALF, c : c + 1], (HALF, 128))
                    for c in range(8)
                ]
                total = [jnp.zeros((HALF, 128), jnp.float32) for _ in range(4)]
                for n in range(7):
                    near = [pack_ref[cell, n, c : c + 1, :] for c in range(8)]
                    rx = own[0] - near[0]
                    ry = own[1] - near[1]
                    rz = own[2] - near[2]
                    dist_sq = rx * rx + ry * ry + rz * rz
                    dist = dist_sq * lax.rsqrt(jnp.maximum(dist_sq, 1e-30))
                    support = jnp.maximum(1.0 - dist, 0.0)
                    cube = support * support * support
                    approach = (
                        (own[3] - near[3]) * rx + (own[4] - near[4]) * ry + (own[5] - near[5]) * rz
                    )
                    inverse = pl.reciprocal(
                        (dist_sq + visc_floor) * (own[6] + near[6]), approx=True
                    )
                    force = (
                        (own[7] + near[7]) - jnp.minimum(approach, 0.0) * inverse
                    ) * cube
                    total[0] = total[0] + force * rx
                    total[1] = total[1] + force * ry
                    total[2] = total[2] + force * rz
                    total[3] = total[3] + cube * approach
                sums = [jnp.sum(t, axis=1, keepdims=True) for t in total]
                merged = jnp.where(
                    lane_half < 2,
                    jnp.where(lane_half < 1, sums[0], sums[1]),
                    jnp.where(lane_half < 3, sums[2], sums[3]),
                )
                base = SLOTS * cell + HALF * half
                res_ref[base : base + HALF, :] = merged
    rates = jnp.transpose(res_ref[...])[0:8]
    scale = -particle_mass * grad_scale
    return rates * jnp.where(row < 3, scale, -scale) - jnp.where(row == 2, gravity, 0.0)


def rates_kernel(grid_ref, out_ref, res_ref, pack_ref):
    level = pl.program_id(0)
    out_ref[0] = level_rates(lambda dz, x: grid_ref[level + dz, x], res_ref, pack_ref)


def rates_call(grid):
    levels = grid.shape[0] - 2
    return pl.pallas_call(
        rates_kernel,
        grid=(levels,),
        out_shape=jax.ShapeDtypeStruct((levels, 8, 128), jnp.float32),
        in_specs=[pl.BlockSpec(grid.shape, lambda k: (0, 0, 0, 0))],
        out_specs=pl.BlockSpec((1, 8, 128), lambda k: (k, 0, 0)),
        scratch_shapes=[
            pltpu.VMEM((128, 128), jnp.float32),
            pltpu.VMEM((4, 7, 8, 128), jnp.float32),
        ],
        compiler_params=pltpu.CompilerParams(vmem_limit_bytes=32 * 1024 * 1024),
    )(grid)


def neighbourhood(own):
    levels = own.shape[0]
    low = shifted(own[:, :, :, 1:2], "tile", 1)
    high = shifted(own[:, :, :, 0:1], "tile", -1)
    wide = jnp.concatenate([low, own, high], axis=3)
    left = shifted(wide[:, :, 1:2], "slab", 1)
    right = shifted(wide[:, :, 0:1], "slab", -1)
    full = jnp.concatenate([left, wide, right], axis=2)
    full = jnp.pad(full, ((1, 1), (0, 0), (0, 0), (0, 0), (0, 0)))
    occ = full[:, 7] > 0.5
    at_x = lax.broadcasted_iota(jnp.int32, occ.shape, 1).astype(jnp.float32)
    at_y = lax.broadcasted_iota(jnp.int32, occ.shape, 2).astype(jnp.float32)
    at_z = lax.broadcasted_iota(jnp.int32, occ.shape, 0).astype(jnp.float32)
    dens = jnp.where(occ, full[:, 6], 1.0)
    dens_2 = dens * dens
    ratio = eos_stiff * (dens_2 * dens_2 * dens_2 * dens - 1.0) / dens_2
    rows = [
        jnp.where(occ, full[:, 0] + at_x, far),
        full[:, 1] + at_y,
        full[:, 2] + at_z,
        full[:, 3],
        full[:, 4],
        full[:, 5],
        dens / visc_scale,
        ratio,
    ]
    rows = jnp.stack([r.reshape(levels + 2, 4, 128) for r in rows], axis=2)
    return rows


def pack_leavers(face_state, face_count, face_leave):
    cell_total = face_count.shape[0] * face_count.shape[1]
    row_total = cell_total * LMAX // 2
    leave_quota = face_leave.reshape(cell_total)
    occupancy = face_count.reshape(cell_total)
    row_ends = jnp.cumsum(leave_quota, dtype=jnp.int32)
    starts = row_ends - leave_quota
    row_ids = jnp.arange(row_total, dtype=jnp.int32)
    owner_mask = (starts[None, :] <= row_ids[:, None]) & (row_ends[None, :] > row_ids[:, None])
    root = jnp.arange(cell_total, dtype=jnp.int32) * SLOTS + occupancy - leave_quota - starts
    source_row = jnp.sum(jnp.where(owner_mask, root[None, :], 0), axis=1, dtype=jnp.int32) + row_ids
    flat_face = face_state.reshape(7, cell_total * SLOTS)
    return jnp.take(flat_face, source_row, axis=1)


def shards(particles, counts, leavers):
    levels = counts.shape[2]
    occ = occupied(counts)
    clean = jnp.where(occ[None], particles, 0.0)
    fields = jnp.concatenate([clean, occ.astype(jnp.float32)[None]], axis=0)
    own = jnp.transpose(fields.reshape(8, 2, 2, levels, SLOTS), (3, 0, 1, 2, 4))
    rates_now = rates_call(neighbourhood(own)).reshape(levels, 8, 2, 2, SLOTS)
    half = 0.5 * time_step
    moved = jnp.concatenate(
        [
            own[:, 0:3] + half * own[:, 3:6],
            own[:, 3:7] + half * rates_now[:, 0:4],
            own[:, 7:8],
        ],
        axis=1,
    )
    rates_mid = rates_call(neighbourhood(moved)).reshape(levels, 8, 2, 2, SLOTS)
    later = own[:, 3:7] + time_step * rates_mid[:, 0:4]
    place = own[:, 0:3] + half * (own[:, 3:6] + later[:, 0:3])
    updated = jnp.concatenate([place, later], axis=1)
    updated = jnp.transpose(updated, (1, 2, 3, 0, 4)).reshape(7, 2, 2, levels * SLOTS)
    remain = counts.at[0].add(-leavers[0, 0]).at[1].add(-leavers[1, 0])
    kept = jnp.where(occupied(remain)[None], updated, 0.0)
    lower_rows = pack_leavers(updated[:, 0], counts[0], leavers[0, 0])
    upper_rows = pack_leavers(updated[:, 1], counts[1], leavers[1, 0])
    from_below = shifted(upper_rows, "slab", 1)
    from_above = shifted(lower_rows, "slab", -1)
    return (kept, jnp.stack([from_below, from_above], axis=0))


def solution(mesh):
    return jax.shard_map(
        shards,
        mesh=mesh,
        in_specs=(
            P(None, "slab", "tile", None),
            P("slab", "tile", None),
            P(None, "slab", "tile", None),
        ),
        out_specs=(P(None, "slab", "tile", None), P(None, None, ("slab", "tile"))),
        check_vma=False,
    )
```

```python
import math

import jax
import jax.numpy as jnp
import numpy as np
from jax import lax
from jax.experimental import pallas as pl
from jax.experimental.pallas import tpu as pltpu
from jax.sharding import PartitionSpec as P

SLOTS = 32
LMAX = 4

sound_speed = 10.0
smoothing = 0.5
kernel_norm = 21.0 / (16.0 * math.pi * smoothing**3)
grad_scale = -5.0 * kernel_norm / (smoothing * smoothing)
eos_stiff = sound_speed * sound_speed / 7.0
particle_mass = 0.125
viscosity = 0.1
visc_floor = 0.01 * smoothing * smoothing
time_step = 0.01
gravity = 9.81
visc_scale = 2.0 * viscosity * sound_speed * smoothing
far = 1.0e6


def shifted(value, axis, steps):
    count = lax.axis_size(axis)
    leading, last = (max(0, -steps), min(count, count - steps))
    return lax.ppermute(value, axis, [(source, source + steps) for source in range(leading, last)])


def occupied(cell_counts):
    filled = jnp.repeat(cell_counts, SLOTS, axis=-1)
    slot_index = jnp.arange(filled.shape[-1], dtype=jnp.int32) % SLOTS
    return slot_index < filled


def selector():
    lane = np.arange(128)
    at_x, at_y = lane // 64, lane // SLOTS % 2
    chosen = np.zeros((3, 16, 9, 128), np.float32)
    for dx in range(3):
        for dy in range(3):
            chosen[:, 4 * (at_x + dx) + at_y + dy, 3 * dx + dy, lane] = 1.0
    return chosen.reshape(48, 9 * 128)


def exchange_kernel(own_ref, out_ref, send_sem, recv_sem, local_sem):
    slab, tile = lax.axis_index("slab"), lax.axis_index("tile")
    slabs, tiles = lax.axis_size("slab"), lax.axis_size("tile")
    barrier = pltpu.get_barrier_semaphore()
    sides = [(a, b) for a in (-1, 0, 1) for b in (-1, 0, 1) if (a, b) != (0, 0)]

    def present(a, b):
        return (
            (slab + a >= 0) & (slab + a < slabs) & (tile + b >= 0) & (tile + b < tiles)
        )

    def copy(n):
        a, b = sides[n]
        source = {-1: pl.ds(0, 1), 0: pl.ds(0, 2), 1: pl.ds(1, 1)}
        target = {-1: pl.ds(3, 1), 0: pl.ds(1, 2), 1: pl.ds(0, 1)}
        return pltpu.make_async_remote_copy(
            src_ref=own_ref.at[source[a], source[b]],
            dst_ref=out_ref.at[target[a], target[b]],
            send_sem=send_sem.at[n],
            recv_sem=recv_sem.at[n],
            device_id=(slab + a, tile + b),
            device_id_type=pl.DeviceIdType.MESH,
        )

    def arrival(n):
        a, b = sides[n]
        source = {-1: pl.ds(0, 1), 0: pl.ds(0, 2), 1: pl.ds(1, 1)}
        target = {-1: pl.ds(3, 1), 0: pl.ds(1, 2), 1: pl.ds(0, 1)}
        return pltpu.make_async_remote_copy(
            src_ref=own_ref.at[source[a], source[b]],
            dst_ref=out_ref.at[target[a], target[b]],
            send_sem=send_sem.at[n],
            recv_sem=recv_sem.at[n],
            device_id=(slab, tile),
            device_id_type=pl.DeviceIdType.MESH,
        )

    count = 0
    for a, b in sides:
        there = present(a, b)
        count = count + there.astype(jnp.int32)

        @pl.when(there)
        def _():
            pl.semaphore_signal(
                barrier,
                inc=1,
                device_id=(slab + a, tile + b),
                device_id_type=pl.DeviceIdType.MESH,
            )

    local = pltpu.make_async_copy(own_ref, out_ref.at[pl.ds(1, 2), pl.ds(1, 2)], local_sem)
    local.start()
    pl.semaphore_wait(barrier, count)
    for n, (a, b) in enumerate(sides):

        @pl.when(present(a, b))
        def _():
            copy(n).start()

    local.wait()
    for n, (a, b) in enumerate(sides):

        @pl.when(present(a, b))
        def _():
            copy(n).wait_send()

        @pl.when(present(-a, -b))
        def _():
            arrival(n).wait_recv()


def exchange(own, number):
    return pl.pallas_call(
        exchange_kernel,
        out_shape=jax.ShapeDtypeStruct((4, 4) + own.shape[2:], jnp.float32),
        in_specs=[pl.BlockSpec(memory_space=pl.ANY)],
        out_specs=pl.BlockSpec(memory_space=pl.ANY),
        scratch_shapes=[
            pltpu.SemaphoreType.DMA((8,)),
            pltpu.SemaphoreType.DMA((8,)),
            pltpu.SemaphoreType.DMA,
        ],
        compiler_params=pltpu.CompilerParams(collective_id=number, has_side_effects=True),
    )(own)


def spread(raw, select):
    lane = lax.broadcasted_iota(jnp.int32, (16, 128), 1)
    column = lax.broadcasted_iota(jnp.int32, (16, 128), 0)
    low, high = raw[:, :128], raw[:, 128:]
    after = pltpu.roll(high, 32, 1)
    before = pltpu.roll(high, 96, 1)
    at_x = ((column // 4) - 1).astype(jnp.float32)
    at_y = ((column % 4) - 1).astype(jnp.float32)
    offset = jnp.where(lane < 32, at_x, jnp.where(lane < 64, at_y, 0.0))
    low = jnp.where((lane < 32) & (after < 0.5), far, low + offset)
    dens = jnp.where(before > 0.5, high, 1.0)
    dens_n = jnp.where(high > 0.5, after, 1.0)
    dens_2 = dens_n * dens_n
    ratio = eos_stiff * (dens_2 * dens_2 * dens_2 * dens_n - 1.0) / dens_2
    high = jnp.where(lane < 64, high, jnp.where(lane < 96, dens * (1.0 / visc_scale), ratio))
    value = jnp.concatenate([low, high], axis=1)
    first = value.astype(jnp.bfloat16).astype(jnp.float32)
    rest = value - first
    second = rest.astype(jnp.bfloat16).astype(jnp.float32)
    third = rest - second
    parts = jnp.transpose(jnp.concatenate([first, second, third], axis=0)).astype(jnp.bfloat16)
    return jnp.dot(parts, select, preferred_element_type=jnp.float32)


def pair_level(levels, slot_mask):
    own = []
    for c in range(8):
        value = levels[1][SLOTS * c : SLOTS * (c + 1), 4 * 128 : 5 * 128]
        own.append(jnp.sum(jnp.where(slot_mask, value, 0.0), axis=0, keepdims=True))
    own = [jnp.broadcast_to(o, (8, 128)) for o in own]
    total = [jnp.zeros((8, 128), jnp.float32) for _ in range(4)]
    for dz in range(3):
        own_z = own[2] + float(1 - dz)
        for d in range(9):
            for j in range(0, SLOTS, 8):
                near = [
                    levels[dz][SLOTS * c + j : SLOTS * c + j + 8, 128 * d : 128 * d + 128]
                    for c in range(8)
                ]
                rx = own[0] - near[0]
                ry = own[1] - near[1]
                rz = own_z - near[2]
                dist_sq = rx * rx + ry * ry + rz * rz
                dist = dist_sq * lax.rsqrt(jnp.maximum(dist_sq, 1e-30))
                support = jnp.maximum(1.0 - dist, 0.0)
                cube = support * support * support
                approach = (
                    (own[3] - near[3]) * rx + (own[4] - near[4]) * ry + (own[5] - near[5]) * rz
                )
                inverse = pl.reciprocal((dist_sq + visc_floor) * (own[6] + near[6]), approx=True)
                force = ((own[7] + near[7]) - jnp.minimum(approach, 0.0) * inverse) * cube
                total[0] = total[0] + force * rx
                total[1] = total[1] + force * ry
                total[2] = total[2] + force * rz
                total[3] = total[3] + cube * approach
    sums = [jnp.sum(t, axis=0, keepdims=True) for t in total]
    row = lax.broadcasted_iota(jnp.int32, (8, 128), 0)
    rates = jnp.where(
        row < 2,
        jnp.where(row < 1, sums[0], sums[1]),
        jnp.where(row < 3, sums[2], sums[3]),
    )
    scale = -particle_mass * grad_scale
    return rates * jnp.where(row < 3, scale, -scale) - jnp.where(row == 2, gravity, 0.0)


def rates_kernel(columns_ref, here_ref, select_ref, out_ref, *spread_refs):
    step = pl.program_id(0)
    count = columns_ref.shape[2]

    def build(level, target):
        at = jnp.clip(level, 0, count - 1)
        raw = jnp.concatenate(
            [columns_ref[x, y, pl.ds(at, 1), :] for x in range(4) for y in range(4)], axis=0
        )
        inside = jnp.where((level >= 0) & (level < count), 1.0, 0.0)
        target[...] = spread(
            jnp.where(here_ref[...] * inside > 0.5, raw, 0.0), select_ref[...]
        )

    @pl.when(step == 0)
    def _():
        build(jnp.int32(-1), spread_refs[0])
        build(jnp.int32(0), spread_refs[1])

    lane = lax.broadcasted_iota(jnp.int32, (SLOTS, 128), 1)
    slot = lax.broadcasted_iota(jnp.int32, (SLOTS, 128), 0)
    slot_mask = lane % SLOTS == slot
    for n in range(4):
        build(step * 4 + n + 1, spread_refs[(n + 2) % 4])
        out_ref[n] = pair_level([spread_refs[(n + i) % 4] for i in range(3)], slot_mask)


def rates_call(columns, here):
    levels = columns.shape[2]
    select = jnp.asarray(selector(), jnp.bfloat16)
    return pl.pallas_call(
        rates_kernel,
        grid=(levels // 4,),
        out_shape=jax.ShapeDtypeStruct((levels, 8, 128), jnp.float32),
        in_specs=[
            pl.BlockSpec(columns.shape, lambda k: (0, 0, 0, 0)),
            pl.BlockSpec(here.shape, lambda k: (0, 0)),
            pl.BlockSpec(select.shape, lambda k: (0, 0)),
        ],
        out_specs=pl.BlockSpec((4, 8, 128), lambda k: (k, 0, 0)),
        scratch_shapes=[pltpu.VMEM((8 * SLOTS, 9 * 128), jnp.float32) for _ in range(4)],
        compiler_params=pltpu.CompilerParams(vmem_limit_bytes=40 * 1024 * 1024),
    )(columns, here, select)


def by_column(rates):
    levels = rates.shape[0]
    return jnp.transpose(rates.reshape(levels, 8, 2, 2, SLOTS)[:, 0:4], (2, 3, 0, 1, 4))


def existing():
    slab, tile = lax.axis_index("slab"), lax.axis_index("tile")
    column = lax.broadcasted_iota(jnp.int32, (16, 256), 0)
    at_x = 2 * slab - 1 + column // 4
    at_y = 2 * tile - 1 + column % 4
    inside = (at_x >= 0) & (at_x < 2 * lax.axis_size("slab"))
    inside = inside & (at_y >= 0) & (at_y < 2 * lax.axis_size("tile"))
    return inside.astype(jnp.float32)


def pack_leavers(face_state, face_count, face_leave):
    cell_total = face_count.shape[0] * face_count.shape[1]
    row_total = cell_total * LMAX // 2
    leave_quota = face_leave.reshape(cell_total)
    occupancy = face_count.reshape(cell_total)
    row_ends = jnp.cumsum(leave_quota, dtype=jnp.int32)
    starts = row_ends - leave_quota
    row_ids = jnp.arange(row_total, dtype=jnp.int32)
    owner_mask = (starts[None, :] <= row_ids[:, None]) & (row_ends[None, :] > row_ids[:, None])
    root = jnp.arange(cell_total, dtype=jnp.int32) * SLOTS + occupancy - leave_quota - starts
    source_row = jnp.sum(jnp.where(owner_mask, root[None, :], 0), axis=1, dtype=jnp.int32) + row_ids
    flat_face = face_state.reshape(7, cell_total * SLOTS)
    return jnp.take(flat_face, source_row, axis=1)


def shards(particles, counts, leavers):
    levels = counts.shape[2]
    occ = occupied(counts)
    clean = jnp.where(occ[None], particles, 0.0)
    fields = jnp.concatenate([clean, occ.astype(jnp.float32)[None]], axis=0)
    own = jnp.transpose(fields.reshape(8, 2, 2, levels, SLOTS), (1, 2, 3, 0, 4))
    here = existing()
    half = 0.5 * time_step
    block = (2, 2, levels, 8 * SLOTS)
    rates_now = by_column(rates_call(exchange(own.reshape(block), 0), here))
    moved = jnp.concatenate(
        [
            own[..., 0:3, :] + half * own[..., 3:6, :],
            own[..., 3:7, :] + half * rates_now,
            own[..., 7:8, :],
        ],
        axis=3,
    )
    moved = jnp.where(own[..., 7:8, :] > 0.5, moved, 0.0)
    rates_mid = by_column(rates_call(exchange(moved.reshape(block), 1), here))
    later = own[..., 3:7, :] + time_step * rates_mid
    place = own[..., 0:3, :] + half * (own[..., 3:6, :] + later[..., 0:3, :])
    updated = jnp.concatenate([place, later], axis=3)
    updated = jnp.transpose(updated, (3, 0, 1, 2, 4)).reshape(7, 2, 2, levels * SLOTS)
    remain = counts.at[0].add(-leavers[0, 0]).at[1].add(-leavers[1, 0])
    kept = jnp.where(occupied(remain)[None], updated, 0.0)
    lower_rows = pack_leavers(updated[:, 0], counts[0], leavers[0, 0])
    upper_rows = pack_leavers(updated[:, 1], counts[1], leavers[1, 0])
    from_below = shifted(upper_rows, "slab", 1)
    from_above = shifted(lower_rows, "slab", -1)
    return (kept, jnp.stack([from_below, from_above], axis=0))


def solution(mesh):
    return jax.shard_map(
        shards,
        mesh=mesh,
        in_specs=(
            P(None, "slab", "tile", None),
            P("slab", "tile", None),
            P(None, "slab", "tile", None),
        ),
        out_specs=(P(None, "slab", "tile", None), P(None, None, ("slab", "tile"))),
        check_vma=False,
    )
```

```python
import functools
import math

import jax
import jax.numpy as jnp
import numpy as np
from jax import lax
from jax.experimental import pallas as pl
from jax.experimental.pallas import tpu as pltpu
from jax.sharding import PartitionSpec as P

SLOTS = 32
LMAX = 4

sound_speed = 10.0
smoothing = 0.5
kernel_norm = 21.0 / (16.0 * math.pi * smoothing**3)
grad_scale = -5.0 * kernel_norm / (smoothing * smoothing)
eos_stiff = sound_speed * sound_speed / 7.0
particle_mass = 0.125
viscosity = 0.1
visc_floor = 0.01 * smoothing * smoothing
time_step = 0.01
gravity = 9.81
visc_scale = 2.0 * viscosity * sound_speed * smoothing
far = 1.0e6


def occupied(cell_counts):
    filled = jnp.repeat(cell_counts, SLOTS, axis=-1)
    slot_index = jnp.arange(filled.shape[-1], dtype=jnp.int32) % SLOTS
    return slot_index < filled


def selector():
    lane = np.arange(128)
    at_x, at_y = lane // 64, lane // SLOTS % 2
    chosen = np.zeros((3, 16, 9, 128), np.float32)
    for dx in range(3):
        for dy in range(3):
            chosen[:, 4 * (at_x + dx) + at_y + dy, 3 * dx + dy, lane] = 1.0
    return chosen.reshape(48, 9 * 128)


def exchange_kernel(own_ref, out_ref, send_sem, recv_sem, local_sem):
    slab, tile = lax.axis_index("slab"), lax.axis_index("tile")
    slabs, tiles = lax.axis_size("slab"), lax.axis_size("tile")
    barrier = pltpu.get_barrier_semaphore()
    sides = [(a, b) for a in (-1, 0, 1) for b in (-1, 0, 1) if (a, b) != (0, 0)]

    def present(a, b):
        return (
            (slab + a >= 0) & (slab + a < slabs) & (tile + b >= 0) & (tile + b < tiles)
        )

    def copy(n, move=1):
        a, b = sides[n]
        source = {-1: pl.ds(0, 1), 0: pl.ds(0, 2), 1: pl.ds(1, 1)}
        target = {-1: pl.ds(3, 1), 0: pl.ds(1, 2), 1: pl.ds(0, 1)}
        return pltpu.make_async_remote_copy(
            src_ref=own_ref.at[source[a], source[b]],
            dst_ref=out_ref.at[target[a], target[b]],
            send_sem=send_sem.at[n],
            recv_sem=recv_sem.at[n],
            device_id=(slab + a * move, tile + b * move),
            device_id_type=pl.DeviceIdType.MESH,
        )

    count = 0
    for a, b in sides:
        there = present(a, b)
        count = count + there.astype(jnp.int32)

        @pl.when(there)
        def _():
            pl.semaphore_signal(
                barrier,
                inc=1,
                device_id=(slab + a, tile + b),
                device_id_type=pl.DeviceIdType.MESH,
            )

    local = pltpu.make_async_copy(own_ref, out_ref.at[pl.ds(1, 2), pl.ds(1, 2)], local_sem)
    local.start()
    pl.semaphore_wait(barrier, count)
    for n, (a, b) in enumerate(sides):

        @pl.when(present(a, b))
        def _():
            copy(n).start()

    local.wait()
    for n, (a, b) in enumerate(sides):

        @pl.when(present(a, b))
        def _():
            copy(n).wait_send()

        @pl.when(present(-a, -b))
        def _():
            copy(n, 0).wait_recv()


def exchange(own, number):
    return pl.pallas_call(
        exchange_kernel,
        out_shape=jax.ShapeDtypeStruct((4, 4) + own.shape[2:], jnp.float32),
        in_specs=[pl.BlockSpec(memory_space=pl.ANY)],
        out_specs=pl.BlockSpec(memory_space=pl.ANY),
        scratch_shapes=[
            pltpu.SemaphoreType.DMA((8,)),
            pltpu.SemaphoreType.DMA((8,)),
            pltpu.SemaphoreType.DMA,
        ],
        compiler_params=pltpu.CompilerParams(collective_id=number, has_side_effects=True),
    )(own)


def migrate_kernel(rows_ref, out_ref, send_sem, recv_sem):
    slab, tile = lax.axis_index("slab"), lax.axis_index("tile")
    has_next, has_last = slab + 1 < lax.axis_size("slab"), slab > 0
    barrier = pltpu.get_barrier_semaphore()

    def copy(source, step):
        return pltpu.make_async_remote_copy(
            src_ref=rows_ref.at[source],
            dst_ref=out_ref.at[1 - source],
            send_sem=send_sem.at[source],
            recv_sem=recv_sem.at[source],
            device_id=(slab + step, tile),
            device_id_type=pl.DeviceIdType.MESH,
        )

    plan = ((1, 1, has_next, has_last), (0, -1, has_last, has_next))
    for source, step, sends, receives in plan:

        @pl.when(sends)
        def _():
            pl.semaphore_signal(
                barrier,
                inc=1,
                device_id=(slab + step, tile),
                device_id_type=pl.DeviceIdType.MESH,
            )

    pl.semaphore_wait(barrier, has_next.astype(jnp.int32) + has_last.astype(jnp.int32))
    for source, step, sends, receives in plan:

        @pl.when(sends)
        def _():
            copy(source, step).start()

        @pl.when(jnp.logical_not(receives))
        def _():
            out_ref[1 - source] = jnp.zeros(out_ref.shape[1:], jnp.float32)

    for source, step, sends, receives in plan:

        @pl.when(sends)
        def _():
            copy(source, step).wait_send()

        @pl.when(receives)
        def _():
            copy(source, 0).wait_recv()


def migrate(rows, number):
    return pl.pallas_call(
        migrate_kernel,
        out_shape=jax.ShapeDtypeStruct(rows.shape, jnp.float32),
        in_specs=[pl.BlockSpec(memory_space=pltpu.VMEM)],
        out_specs=pl.BlockSpec(memory_space=pltpu.VMEM),
        scratch_shapes=[pltpu.SemaphoreType.DMA((2,)), pltpu.SemaphoreType.DMA((2,))],
        compiler_params=pltpu.CompilerParams(collective_id=number, has_side_effects=True),
    )(rows)


def column_parts(low, high):
    lane = lax.broadcasted_iota(jnp.int32, (16, 128), 1)
    column = lax.broadcasted_iota(jnp.int32, (16, 128), 0)
    occ = pltpu.roll(low, 32, 1)
    at_x = ((column // 4) - 1).astype(jnp.float32)
    at_y = ((column % 4) - 1).astype(jnp.float32)
    offset = jnp.where(lane < 32, at_x, jnp.where(lane < 64, at_y, 0.0))
    dens = jnp.where(low > 0.5, high, 1.0)
    dens_2 = dens * dens
    ratio = eos_stiff * (dens_2 * dens_2 * dens_2 * dens - 1.0) / dens_2
    low = jnp.where((lane < 32) & (occ < 0.5), far, low + offset)
    low = jnp.where(lane < 96, low, ratio)
    high = jnp.where(lane < 96, high, dens * (1.0 / visc_scale))
    value = jnp.concatenate([low, high], axis=1)
    first = value.astype(jnp.bfloat16).astype(jnp.float32)
    rest = value - first
    second = rest.astype(jnp.bfloat16).astype(jnp.float32)
    third = rest - second
    return jnp.transpose(jnp.concatenate([first, second, third], axis=0)).astype(jnp.bfloat16)


def pair_level(levels, slot_mask, between):
    own = []
    for c in range(8):
        value = levels[1][SLOTS * c : SLOTS * (c + 1), 4 * 128 : 5 * 128]
        own.append(jnp.sum(jnp.where(slot_mask, value, 0.0), axis=0, keepdims=True))
    own = [jnp.broadcast_to(o, (8, 128)) for o in own]
    total = [jnp.zeros((8, 128), jnp.float32) for _ in range(4)]
    for dz in range(3):
        own_z = own[2] + float(1 - dz)
        for d in range(9):
            between(9 * dz + d)
            for j in range(0, SLOTS, 8):
                near = [
                    levels[dz][SLOTS * c + j : SLOTS * c + j + 8, 128 * d : 128 * d + 128]
                    for c in range(8)
                ]
                rx = own[0] - near[0]
                ry = own[1] - near[1]
                rz = own_z - near[2]
                dist_sq = rx * rx + ry * ry + rz * rz
                dist = dist_sq * lax.rsqrt(jnp.maximum(dist_sq, 1e-30))
                support = jnp.maximum(1.0 - dist, 0.0)
                cube = support * support * support
                approach = (
                    (own[4] - near[4]) * rx + (own[5] - near[5]) * ry + (own[6] - near[6]) * rz
                )
                inverse = pl.reciprocal((dist_sq + visc_floor) * (own[7] + near[7]), approx=True)
                force = ((own[3] + near[3]) - jnp.minimum(approach, 0.0) * inverse) * cube
                total[0] = total[0] + force * rx
                total[1] = total[1] + force * ry
                total[2] = total[2] + force * rz
                total[3] = total[3] + cube * approach
    sums = [jnp.sum(t, axis=0, keepdims=True) for t in total]
    row = lax.broadcasted_iota(jnp.int32, (8, 128), 0)
    rates = jnp.where(
        row < 2,
        jnp.where(row < 1, sums[0], sums[1]),
        jnp.where(row < 3, sums[2], sums[3]),
    )
    scale = -particle_mass * grad_scale
    return rates * jnp.where(row < 3, scale, -scale) - jnp.where(row == 2, gravity, 0.0)


def rates_kernel(later, *refs):
    columns_ref = refs[0]
    later_ref = refs[1] if later else None
    here_ref, select_ref, out_ref, *scratch = refs[1 + later :]
    parts_refs, spread_refs = scratch[:2], scratch[2:]
    step = pl.program_id(0)
    count = columns_ref.shape[2]

    def prepare(level, parts_ref):
        at = jnp.clip(level, 0, count - 1)

        def rows(ref):
            return jnp.concatenate(
                [ref[x, y, pl.ds(at, 1), :] for x in range(4) for y in range(4)], axis=0
            )

        inside = jnp.where((level >= 0) & (level < count), 1.0, 0.0)
        valid = here_ref[...] * inside > 0.5
        raw = jnp.where(valid, rows(columns_ref), 0.0)
        low, high = raw[:, :128], raw[:, 128:]
        if later:
            lane = lax.broadcasted_iota(jnp.int32, (16, 128), 1)
            low = low + 0.5 * time_step * jnp.where(lane < 96, high, 0.0)
            high = jnp.where(valid[:, :128], rows(later_ref), 0.0)
        parts_ref[...] = column_parts(low, high)

    def fill(n, parts_ref, target):
        tile = slice(256 * n, min(256 * n + 256, 9 * 128))
        target[:, tile] = jnp.dot(
            parts_ref[...], select_ref[:, tile], preferred_element_type=jnp.float32
        )

    @pl.when(step == 0)
    def _():
        for n in range(3):
            prepare(jnp.int32(n - 1), parts_refs[0])
            for tile in range(5):
                fill(tile, parts_refs[0], spread_refs[n])

    lane = lax.broadcasted_iota(jnp.int32, (SLOTS, 128), 1)
    slot = lax.broadcasted_iota(jnp.int32, (SLOTS, 128), 0)
    slot_mask = lane % SLOTS == slot
    for n in range(4):

        def between(place):
            if place == 0:
                prepare(step * 4 + n + 2, parts_refs[n % 2])
            elif place % 5 == 4:
                fill(place // 5, parts_refs[n % 2], spread_refs[(n + 3) % 4])

        out_ref[n] = pair_level([spread_refs[(n + i) % 4] for i in range(3)], slot_mask, between)


def rates_call(columns, here, later=None):
    levels = columns.shape[2]
    select = jnp.asarray(selector(), jnp.bfloat16)
    arrays = [columns] + ([] if later is None else [later])
    return pl.pallas_call(
        functools.partial(rates_kernel, later is not None),
        grid=(levels // 4,),
        out_shape=jax.ShapeDtypeStruct((levels, 8, 128), jnp.float32),
        in_specs=[pl.BlockSpec(a.shape, lambda k: (0, 0, 0, 0)) for a in arrays]
        + [
            pl.BlockSpec(here.shape, lambda k: (0, 0)),
            pl.BlockSpec(select.shape, lambda k: (0, 0)),
        ],
        out_specs=pl.BlockSpec((4, 8, 128), lambda k: (k, 0, 0)),
        scratch_shapes=[pltpu.VMEM((8 * SLOTS, 48), jnp.bfloat16) for _ in range(2)]
        + [pltpu.VMEM((8 * SLOTS, 9 * 128), jnp.float32) for _ in range(4)],
        compiler_params=pltpu.CompilerParams(vmem_limit_bytes=40 * 1024 * 1024),
    )(*arrays, here, select)


def by_column(rates):
    levels = rates.shape[0]
    return jnp.transpose(rates.reshape(levels, 8, 2, 2, SLOTS)[:, 0:4], (2, 3, 0, 1, 4))


def existing():
    slab, tile = lax.axis_index("slab"), lax.axis_index("tile")
    column = lax.broadcasted_iota(jnp.int32, (16, 256), 0)
    at_x = 2 * slab - 1 + column // 4
    at_y = 2 * tile - 1 + column % 4
    inside = (at_x >= 0) & (at_x < 2 * lax.axis_size("slab"))
    inside = inside & (at_y >= 0) & (at_y < 2 * lax.axis_size("tile"))
    return inside.astype(jnp.float32)


def pack_leavers(face_state, face_count, face_leave):
    cell_total = face_count.shape[0] * face_count.shape[1]
    row_total = cell_total * LMAX // 2
    leave_quota = face_leave.reshape(cell_total)
    occupancy = face_count.reshape(cell_total)
    row_ends = jnp.cumsum(leave_quota, dtype=jnp.int32)
    starts = row_ends - leave_quota
    row_ids = jnp.arange(row_total, dtype=jnp.int32)
    owner_mask = (starts[None, :] <= row_ids[:, None]) & (row_ends[None, :] > row_ids[:, None])
    root = jnp.arange(cell_total, dtype=jnp.int32) * SLOTS + occupancy - leave_quota - starts
    source_row = jnp.sum(jnp.where(owner_mask, root[None, :], 0), axis=1, dtype=jnp.int32) + row_ids
    flat_face = face_state.reshape(7, cell_total * SLOTS)
    return jnp.take(flat_face, source_row, axis=1)


def shards(particles, counts, leavers):
    levels = counts.shape[2]
    occ = occupied(counts)
    clean = jnp.where(occ[None], particles, 0.0)
    fields = jnp.concatenate([clean[0:3], occ.astype(jnp.float32)[None], clean[3:7]], axis=0)
    own = jnp.transpose(fields.reshape(8, 2, 2, levels, SLOTS), (1, 2, 3, 0, 4))
    here = existing()
    half = 0.5 * time_step
    columns = exchange(own.reshape(2, 2, levels, 8 * SLOTS), 0)
    rates_now = by_column(rates_call(columns, here))
    moved = jnp.where(own[..., 3:4, :] > 0.5, own[..., 4:8, :] + half * rates_now, 0.0)
    later = exchange(moved.reshape(2, 2, levels, 4 * SLOTS), 1)
    rates_mid = by_column(rates_call(columns, here, later))
    speed = own[..., 4:8, :] + time_step * rates_mid
    place = own[..., 0:3, :] + half * (own[..., 4:7, :] + speed[..., 0:3, :])
    updated = jnp.concatenate([place, speed], axis=3)
    updated = jnp.transpose(updated, (3, 0, 1, 2, 4)).reshape(7, 2, 2, levels * SLOTS)
    remain = counts.at[0].add(-leavers[0, 0]).at[1].add(-leavers[1, 0])
    kept = jnp.where(occupied(remain)[None], updated, 0.0)
    rows = jnp.stack([pack_leavers(updated[:, f], counts[f], leavers[f, 0]) for f in range(2)])
    return (kept, migrate(rows, 2))


def solution(mesh):
    return jax.shard_map(
        shards,
        mesh=mesh,
        in_specs=(
            P(None, "slab", "tile", None),
            P("slab", "tile", None),
            P(None, "slab", "tile", None),
        ),
        out_specs=(P(None, "slab", "tile", None), P(None, None, ("slab", "tile"))),
        check_vma=False,
    )
```

```python
import functools
import math

import jax
import jax.numpy as jnp
import numpy as np
from jax import lax
from jax.experimental import pallas as pl
from jax.experimental.pallas import tpu as pltpu
from jax.sharding import PartitionSpec as P

SLOTS = 32
LMAX = 4

sound_speed = 10.0
smoothing = 0.5
kernel_norm = 21.0 / (16.0 * math.pi * smoothing**3)
grad_scale = -5.0 * kernel_norm / (smoothing * smoothing)
eos_stiff = sound_speed * sound_speed / 7.0
particle_mass = 0.125
viscosity = 0.1
visc_floor = 0.01 * smoothing * smoothing
time_step = 0.01
gravity = 9.81
visc_scale = 2.0 * viscosity * sound_speed * smoothing
far = 1.0e6


def occupied(cell_counts):
    filled = jnp.repeat(cell_counts, SLOTS, axis=-1)
    slot_index = jnp.arange(filled.shape[-1], dtype=jnp.int32) % SLOTS
    return slot_index < filled


def selector():
    lane = np.arange(128)
    at_x, at_y = lane // 64, lane // SLOTS % 2
    chosen = np.zeros((3, 16, 9, 128), np.float32)
    for dx in range(3):
        for dy in range(3):
            chosen[:, 4 * (at_x + dx) + at_y + dy, 3 * dx + dy, lane] = 1.0
    return chosen.reshape(48, 9 * 128)


def exchange_kernel(own_ref, out_ref, send_sem, recv_sem, local_sem):
    slab, tile = lax.axis_index("slab"), lax.axis_index("tile")
    slabs, tiles = lax.axis_size("slab"), lax.axis_size("tile")
    barrier = pltpu.get_barrier_semaphore()
    sides = [(a, b) for a in (-1, 0, 1) for b in (-1, 0, 1) if (a, b) != (0, 0)]

    def present(a, b):
        return (
            (slab + a >= 0) & (slab + a < slabs) & (tile + b >= 0) & (tile + b < tiles)
        )

    def copy(n, move=1):
        a, b = sides[n]
        source = {-1: pl.ds(0, 1), 0: pl.ds(0, 2), 1: pl.ds(1, 1)}
        target = {-1: pl.ds(3, 1), 0: pl.ds(1, 2), 1: pl.ds(0, 1)}
        return pltpu.make_async_remote_copy(
            src_ref=own_ref.at[source[a], source[b]],
            dst_ref=out_ref.at[target[a], target[b]],
            send_sem=send_sem.at[n],
            recv_sem=recv_sem.at[n],
            device_id=(slab + a * move, tile + b * move),
            device_id_type=pl.DeviceIdType.MESH,
        )

    count = 0
    for a, b in sides:
        there = present(a, b)
        count = count + there.astype(jnp.int32)

        @pl.when(there)
        def _():
            pl.semaphore_signal(
                barrier,
                inc=1,
                device_id=(slab + a, tile + b),
                device_id_type=pl.DeviceIdType.MESH,
            )

    local = pltpu.make_async_copy(own_ref, out_ref.at[pl.ds(1, 2), pl.ds(1, 2)], local_sem)
    local.start()
    pl.semaphore_wait(barrier, count)
    for n, (a, b) in enumerate(sides):

        @pl.when(present(a, b))
        def _():
            copy(n).start()

    local.wait()
    for n, (a, b) in enumerate(sides):

        @pl.when(present(a, b))
        def _():
            copy(n).wait_send()

        @pl.when(present(-a, -b))
        def _():
            copy(n, 0).wait_recv()


def exchange(own, number):
    return pl.pallas_call(
        exchange_kernel,
        out_shape=jax.ShapeDtypeStruct((4, 4) + own.shape[2:], jnp.float32),
        in_specs=[pl.BlockSpec(memory_space=pl.ANY)],
        out_specs=pl.BlockSpec(memory_space=pl.ANY),
        scratch_shapes=[
            pltpu.SemaphoreType.DMA((8,)),
            pltpu.SemaphoreType.DMA((8,)),
            pltpu.SemaphoreType.DMA,
        ],
        compiler_params=pltpu.CompilerParams(collective_id=number, has_side_effects=True),
    )(own)


def migrate_kernel(rows_ref, out_ref, send_sem, recv_sem):
    slab, tile = lax.axis_index("slab"), lax.axis_index("tile")
    has_next, has_last = slab + 1 < lax.axis_size("slab"), slab > 0
    barrier = pltpu.get_barrier_semaphore()

    def copy(source, step):
        return pltpu.make_async_remote_copy(
            src_ref=rows_ref.at[source],
            dst_ref=out_ref.at[1 - source],
            send_sem=send_sem.at[source],
            recv_sem=recv_sem.at[source],
            device_id=(slab + step, tile),
            device_id_type=pl.DeviceIdType.MESH,
        )

    plan = ((1, 1, has_next, has_last), (0, -1, has_last, has_next))
    for source, step, sends, receives in plan:

        @pl.when(sends)
        def _():
            pl.semaphore_signal(
                barrier,
                inc=1,
                device_id=(slab + step, tile),
                device_id_type=pl.DeviceIdType.MESH,
            )

    pl.semaphore_wait(barrier, has_next.astype(jnp.int32) + has_last.astype(jnp.int32))
    for source, step, sends, receives in plan:

        @pl.when(sends)
        def _():
            copy(source, step).start()

        @pl.when(jnp.logical_not(receives))
        def _():
            out_ref[1 - source] = jnp.zeros(out_ref.shape[1:], jnp.float32)

    for source, step, sends, receives in plan:

        @pl.when(sends)
        def _():
            copy(source, step).wait_send()

        @pl.when(receives)
        def _():
            copy(source, 0).wait_recv()


def migrate(rows, number):
    return pl.pallas_call(
        migrate_kernel,
        out_shape=jax.ShapeDtypeStruct(rows.shape, jnp.float32),
        in_specs=[pl.BlockSpec(memory_space=pltpu.VMEM)],
        out_specs=pl.BlockSpec(memory_space=pltpu.VMEM),
        scratch_shapes=[pltpu.SemaphoreType.DMA((2,)), pltpu.SemaphoreType.DMA((2,))],
        compiler_params=pltpu.CompilerParams(collective_id=number, has_side_effects=True),
    )(rows)


def column_parts(low, high):
    lane = lax.broadcasted_iota(jnp.int32, (16, 128), 1)
    column = lax.broadcasted_iota(jnp.int32, (16, 128), 0)
    occ = pltpu.roll(low, 32, 1)
    at_x = ((column // 4) - 1).astype(jnp.float32)
    at_y = ((column % 4) - 1).astype(jnp.float32)
    offset = jnp.where(lane < 32, at_x, jnp.where(lane < 64, at_y, 0.0))
    dens = jnp.where(low > 0.5, high, 1.0)
    dens_2 = dens * dens
    ratio = eos_stiff * (dens_2 * dens_2 * dens_2 * dens - 1.0) / dens_2
    low = jnp.where((lane < 32) & (occ < 0.5), far, low + offset)
    low = jnp.where(lane < 96, low, ratio)
    high = jnp.where(lane < 96, high, dens * (1.0 / visc_scale))
    value = jnp.concatenate([low, high], axis=1)
    first = value.astype(jnp.bfloat16).astype(jnp.float32)
    rest = value - first
    second = rest.astype(jnp.bfloat16).astype(jnp.float32)
    third = rest - second
    return jnp.transpose(jnp.concatenate([first, second, third], axis=0)).astype(jnp.bfloat16)


def pair_level(levels, slot_mask, between):
    own = []
    for c in range(8):
        value = levels[1][SLOTS * c : SLOTS * (c + 1), 4 * 128 : 5 * 128]
        own.append(jnp.sum(jnp.where(slot_mask, value, 0.0), axis=0, keepdims=True))
    own = [jnp.broadcast_to(o, (8, 128)) for o in own]
    total = [jnp.zeros((8, 128), jnp.float32) for _ in range(4)]
    for dz in range(3):
        own_z = own[2] + float(1 - dz)
        for d in range(9):
            between(9 * dz + d)
            near = [
                levels[dz][SLOTS * c : SLOTS * (c + 1), 128 * d : 128 * d + 128].reshape(4, 8, 128)
                for c in range(8)
            ]
            rx = own[0] - near[0]
            ry = own[1] - near[1]
            rz = own_z - near[2]
            dist_sq = rx * rx + ry * ry + rz * rz
            dist = dist_sq * lax.rsqrt(jnp.maximum(dist_sq, 1e-30))
            support = jnp.maximum(1.0 - dist, 0.0)
            cube = support * support * support
            approach = (own[4] - near[4]) * rx + (own[5] - near[5]) * ry + (own[6] - near[6]) * rz
            inverse = pl.reciprocal((dist_sq + visc_floor) * (own[7] + near[7]), approx=True)
            force = ((own[3] + near[3]) - jnp.minimum(approach, 0.0) * inverse) * cube
            for t, term in enumerate((force * rx, force * ry, force * rz, cube * approach)):
                total[t] = total[t] + jnp.sum(term, axis=0)
    sums = [jnp.sum(t, axis=0, keepdims=True) for t in total]
    row = lax.broadcasted_iota(jnp.int32, (8, 128), 0)
    rates = jnp.where(
        row < 2,
        jnp.where(row < 1, sums[0], sums[1]),
        jnp.where(row < 3, sums[2], sums[3]),
    )
    scale = -particle_mass * grad_scale
    return rates * jnp.where(row < 3, scale, -scale) - jnp.where(row == 2, gravity, 0.0)


def rates_kernel(later, *refs):
    columns_ref = refs[0]
    later_ref = refs[1] if later else None
    here_ref, select_ref, out_ref, *scratch = refs[1 + later :]
    parts_refs, spread_refs = scratch[:2], scratch[2:]
    step = pl.program_id(0)
    count = columns_ref.shape[2]

    def prepare(level, parts_ref):
        at = jnp.clip(level, 0, count - 1)

        def rows(ref):
            return jnp.concatenate(
                [ref[x, y, pl.ds(at, 1), :] for x in range(4) for y in range(4)], axis=0
            )

        inside = jnp.where((level >= 0) & (level < count), 1.0, 0.0)
        valid = here_ref[...] * inside > 0.5
        raw = jnp.where(valid, rows(columns_ref), 0.0)
        low, high = raw[:, :128], raw[:, 128:]
        if later:
            lane = lax.broadcasted_iota(jnp.int32, (16, 128), 1)
            low = low + 0.5 * time_step * jnp.where(lane < 96, high, 0.0)
            high = jnp.where(valid[:, :128], rows(later_ref), 0.0)
        parts_ref[...] = column_parts(low, high)

    def fill(n, parts_ref, target):
        tile = slice(256 * n, min(256 * n + 256, 9 * 128))
        target[:, tile] = jnp.dot(
            parts_ref[...], select_ref[:, tile], preferred_element_type=jnp.float32
        )

    @pl.when(step == 0)
    def _():
        for n in range(3):
            prepare(jnp.int32(n - 1), parts_refs[0])
            for tile in range(5):
                fill(tile, parts_refs[0], spread_refs[n])

    lane = lax.broadcasted_iota(jnp.int32, (SLOTS, 128), 1)
    slot = lax.broadcasted_iota(jnp.int32, (SLOTS, 128), 0)
    slot_mask = lane % SLOTS == slot
    for n in range(4):

        def between(place):
            if place == 0:
                prepare(step * 4 + n + 2, parts_refs[n % 2])
            elif place % 5 == 4:
                fill(place // 5, parts_refs[n % 2], spread_refs[(n + 3) % 4])

        out_ref[n] = pair_level([spread_refs[(n + i) % 4] for i in range(3)], slot_mask, between)


def rates_call(columns, here, later=None):
    levels = columns.shape[2]
    select = jnp.asarray(selector(), jnp.bfloat16)
    arrays = [columns] + ([] if later is None else [later])
    return pl.pallas_call(
        functools.partial(rates_kernel, later is not None),
        grid=(levels // 4,),
        out_shape=jax.ShapeDtypeStruct((levels, 8, 128), jnp.float32),
        in_specs=[pl.BlockSpec(a.shape, lambda k: (0, 0, 0, 0)) for a in arrays]
        + [
            pl.BlockSpec(here.shape, lambda k: (0, 0)),
            pl.BlockSpec(select.shape, lambda k: (0, 0)),
        ],
        out_specs=pl.BlockSpec((4, 8, 128), lambda k: (k, 0, 0)),
        scratch_shapes=[pltpu.VMEM((8 * SLOTS, 48), jnp.bfloat16) for _ in range(2)]
        + [pltpu.VMEM((8 * SLOTS, 9 * 128), jnp.float32) for _ in range(4)],
        compiler_params=pltpu.CompilerParams(vmem_limit_bytes=40 * 1024 * 1024),
    )(*arrays, here, select)


def by_column(rates):
    levels = rates.shape[0]
    return jnp.transpose(rates.reshape(levels, 8, 2, 2, SLOTS)[:, 0:4], (2, 3, 0, 1, 4))


def existing():
    slab, tile = lax.axis_index("slab"), lax.axis_index("tile")
    column = lax.broadcasted_iota(jnp.int32, (16, 256), 0)
    at_x = 2 * slab - 1 + column // 4
    at_y = 2 * tile - 1 + column % 4
    inside = (at_x >= 0) & (at_x < 2 * lax.axis_size("slab"))
    inside = inside & (at_y >= 0) & (at_y < 2 * lax.axis_size("tile"))
    return inside.astype(jnp.float32)


def pack_leavers(face_state, face_count, face_leave):
    cell_total = face_count.shape[0] * face_count.shape[1]
    row_total = cell_total * LMAX // 2
    leave_quota = face_leave.reshape(cell_total)
    occupancy = face_count.reshape(cell_total)
    row_ends = jnp.cumsum(leave_quota, dtype=jnp.int32)
    starts = row_ends - leave_quota
    row_ids = jnp.arange(row_total, dtype=jnp.int32)
    owner_mask = (starts[None, :] <= row_ids[:, None]) & (row_ends[None, :] > row_ids[:, None])
    root = jnp.arange(cell_total, dtype=jnp.int32) * SLOTS + occupancy - leave_quota - starts
    source_row = jnp.sum(jnp.where(owner_mask, root[None, :], 0), axis=1, dtype=jnp.int32) + row_ids
    flat_face = face_state.reshape(7, cell_total * SLOTS)
    return jnp.take(flat_face, source_row, axis=1)


def shards(particles, counts, leavers):
    levels = counts.shape[2]
    occ = occupied(counts)
    clean = jnp.where(occ[None], particles, 0.0)
    fields = jnp.concatenate([clean[0:3], occ.astype(jnp.float32)[None], clean[3:7]], axis=0)
    own = jnp.transpose(fields.reshape(8, 2, 2, levels, SLOTS), (1, 2, 3, 0, 4))
    here = existing()
    half = 0.5 * time_step
    columns = exchange(own.reshape(2, 2, levels, 8 * SLOTS), 0)
    rates_now = by_column(rates_call(columns, here))
    moved = jnp.where(own[..., 3:4, :] > 0.5, own[..., 4:8, :] + half * rates_now, 0.0)
    later = exchange(moved.reshape(2, 2, levels, 4 * SLOTS), 1)
    rates_mid = by_column(rates_call(columns, here, later))
    speed = own[..., 4:8, :] + time_step * rates_mid
    place = own[..., 0:3, :] + half * (own[..., 4:7, :] + speed[..., 0:3, :])
    updated = jnp.concatenate([place, speed], axis=3)
    updated = jnp.transpose(updated, (3, 0, 1, 2, 4)).reshape(7, 2, 2, levels * SLOTS)
    remain = counts.at[0].add(-leavers[0, 0]).at[1].add(-leavers[1, 0])
    kept = jnp.where(occupied(remain)[None], updated, 0.0)
    rows = jnp.stack([pack_leavers(updated[:, f], counts[f], leavers[f, 0]) for f in range(2)])
    return (kept, migrate(rows, 2))


def solution(mesh):
    return jax.shard_map(
        shards,
        mesh=mesh,
        in_specs=(
            P(None, "slab", "tile", None),
            P("slab", "tile", None),
            P(None, "slab", "tile", None),
        ),
        out_specs=(P(None, "slab", "tile", None), P(None, None, ("slab", "tile"))),
        check_vma=False,
    )
```

```python
import functools
import math

import jax
import jax.numpy as jnp
import numpy as np
from jax import lax
from jax.experimental import pallas as pl
from jax.experimental.pallas import tpu as pltpu
from jax.sharding import PartitionSpec as P

SLOTS = 32
LMAX = 4

sound_speed = 10.0
smoothing = 0.5
kernel_norm = 21.0 / (16.0 * math.pi * smoothing**3)
grad_scale = -5.0 * kernel_norm / (smoothing * smoothing)
eos_stiff = sound_speed * sound_speed / 7.0
particle_mass = 0.125
viscosity = 0.1
visc_floor = 0.01 * smoothing * smoothing
time_step = 0.01
gravity = 9.81
visc_scale = 2.0 * viscosity * sound_speed * smoothing
far = 1.0e6


def occupied(cell_counts):
    filled = jnp.repeat(cell_counts, SLOTS, axis=-1)
    slot_index = jnp.arange(filled.shape[-1], dtype=jnp.int32) % SLOTS
    return slot_index < filled


def selector():
    lane = np.arange(128)
    at_x, at_y = lane // 64, lane // SLOTS % 2
    chosen = np.zeros((3, 16, 9, 128), np.float32)
    for dx in range(3):
        for dy in range(3):
            chosen[:, 4 * (at_x + dx) + at_y + dy, 3 * dx + dy, lane] = 1.0
    return chosen.reshape(48, 9 * 128)


def exchange_kernel(own_ref, out_ref, send_sem, recv_sem, local_sem):
    slab, tile = lax.axis_index("slab"), lax.axis_index("tile")
    slabs, tiles = lax.axis_size("slab"), lax.axis_size("tile")
    barrier = pltpu.get_barrier_semaphore()
    sides = [(-1, 0), (1, 0), (0, -1), (0, 1), (-1, -1), (-1, 1), (1, -1), (1, 1)]

    def present(a, b):
        return (
            (slab + a >= 0) & (slab + a < slabs) & (tile + b >= 0) & (tile + b < tiles)
        )

    def copy(n, move=1):
        a, b = sides[n]
        source = {-1: pl.ds(0, 1), 0: pl.ds(0, 2), 1: pl.ds(1, 1)}
        held = {-1: pl.ds(1, 1), 1: pl.ds(2, 1)}
        target = {-1: pl.ds(3, 1), 0: pl.ds(1, 2), 1: pl.ds(0, 1)}
        corner = a != 0 and b != 0
        if corner:
            block, step = out_ref.at[target[a], held[b]], (0, b)
        else:
            block, step = own_ref.at[source[a], source[b]], (a, b)
        return pltpu.make_async_remote_copy(
            src_ref=block,
            dst_ref=out_ref.at[target[a], target[b]],
            send_sem=send_sem.at[n],
            recv_sem=recv_sem.at[n],
            device_id=(slab + step[0] * move, tile + step[1] * move),
            device_id_type=pl.DeviceIdType.MESH,
        )

    count = 0
    for a, b in sides[:4]:
        there = present(a, b)
        count = count + there.astype(jnp.int32)

        @pl.when(there)
        def _():
            pl.semaphore_signal(
                barrier,
                inc=1,
                device_id=(slab + a, tile + b),
                device_id_type=pl.DeviceIdType.MESH,
            )

    local = pltpu.make_async_copy(own_ref, out_ref.at[pl.ds(1, 2), pl.ds(1, 2)], local_sem)
    local.start()
    pl.semaphore_wait(barrier, count)
    for n, (a, b) in enumerate(sides[:4]):

        @pl.when(present(a, b))
        def _():
            copy(n).start()

    for n, (a, b) in enumerate(sides[:2]):

        @pl.when(present(-a, 0))
        def _():
            copy(n, 0).wait_recv()

        for m in range(4, 8):
            if sides[m][0] == a:

                @pl.when(present(-a, 0) & present(0, sides[m][1]))
                def _():
                    copy(m).start()

    local.wait()
    for n, (a, b) in enumerate(sides):

        @pl.when(present(a, b) if n < 4 else present(-a, 0) & present(0, b))
        def _():
            copy(n).wait_send()

        if n >= 2:

            @pl.when(present(-a, -b))
            def _():
                copy(n, 0).wait_recv()


def exchange(own, number):
    return pl.pallas_call(
        exchange_kernel,
        out_shape=jax.ShapeDtypeStruct((4, 4) + own.shape[2:], jnp.float32),
        in_specs=[pl.BlockSpec(memory_space=pl.ANY)],
        out_specs=pl.BlockSpec(memory_space=pl.ANY),
        scratch_shapes=[
            pltpu.SemaphoreType.DMA((8,)),
            pltpu.SemaphoreType.DMA((8,)),
            pltpu.SemaphoreType.DMA,
        ],
        compiler_params=pltpu.CompilerParams(collective_id=number, has_side_effects=True),
    )(own)


def migrate_kernel(rows_ref, out_ref, send_sem, recv_sem):
    slab, tile = lax.axis_index("slab"), lax.axis_index("tile")
    has_next, has_last = slab + 1 < lax.axis_size("slab"), slab > 0
    barrier = pltpu.get_barrier_semaphore()

    def copy(source, step):
        return pltpu.make_async_remote_copy(
            src_ref=rows_ref.at[source],
            dst_ref=out_ref.at[1 - source],
            send_sem=send_sem.at[source],
            recv_sem=recv_sem.at[source],
            device_id=(slab + step, tile),
            device_id_type=pl.DeviceIdType.MESH,
        )

    plan = ((1, 1, has_next, has_last), (0, -1, has_last, has_next))
    for source, step, sends, receives in plan:

        @pl.when(sends)
        def _():
            pl.semaphore_signal(
                barrier,
                inc=1,
                device_id=(slab + step, tile),
                device_id_type=pl.DeviceIdType.MESH,
            )

    pl.semaphore_wait(barrier, has_next.astype(jnp.int32) + has_last.astype(jnp.int32))
    for source, step, sends, receives in plan:

        @pl.when(sends)
        def _():
            copy(source, step).start()

        @pl.when(jnp.logical_not(receives))
        def _():
            out_ref[1 - source] = jnp.zeros(out_ref.shape[1:], jnp.float32)

    for source, step, sends, receives in plan:

        @pl.when(sends)
        def _():
            copy(source, step).wait_send()

        @pl.when(receives)
        def _():
            copy(source, 0).wait_recv()


def migrate(rows, number):
    return pl.pallas_call(
        migrate_kernel,
        out_shape=jax.ShapeDtypeStruct(rows.shape, jnp.float32),
        in_specs=[pl.BlockSpec(memory_space=pltpu.VMEM)],
        out_specs=pl.BlockSpec(memory_space=pltpu.VMEM),
        scratch_shapes=[pltpu.SemaphoreType.DMA((2,)), pltpu.SemaphoreType.DMA((2,))],
        compiler_params=pltpu.CompilerParams(collective_id=number, has_side_effects=True),
    )(rows)


def column_parts(low, high):
    lane = lax.broadcasted_iota(jnp.int32, (16, 128), 1)
    column = lax.broadcasted_iota(jnp.int32, (16, 128), 0)
    occ = pltpu.roll(low, 32, 1)
    at_x = ((column // 4) - 1).astype(jnp.float32)
    at_y = ((column % 4) - 1).astype(jnp.float32)
    offset = jnp.where(lane < 32, at_x, jnp.where(lane < 64, at_y, 0.0))
    dens = jnp.where(low > 0.5, high, 1.0)
    dens_2 = dens * dens
    ratio = eos_stiff * (dens_2 * dens_2 * dens_2 * dens - 1.0) / dens_2
    low = jnp.where((lane < 32) & (occ < 0.5), far, low + offset)
    low = jnp.where(lane < 96, low, ratio)
    high = jnp.where(lane < 96, high, dens * (1.0 / visc_scale))
    value = jnp.concatenate([low, high], axis=1)
    first = value.astype(jnp.bfloat16).astype(jnp.float32)
    rest = value - first
    second = rest.astype(jnp.bfloat16).astype(jnp.float32)
    third = rest - second
    return jnp.transpose(jnp.concatenate([first, second, third], axis=0)).astype(jnp.bfloat16)


def pair_level(levels, slot_mask, between):
    own = []
    for c in range(8):
        value = levels[1][SLOTS * c : SLOTS * (c + 1), 4 * 128 : 5 * 128]
        own.append(jnp.sum(jnp.where(slot_mask, value, 0.0), axis=0, keepdims=True))
    own = [jnp.broadcast_to(o, (8, 128)) for o in own]
    total = [jnp.zeros((8, 128), jnp.float32) for _ in range(4)]
    for dz in range(3):
        own_z = own[2] + float(1 - dz)
        for d in range(9):
            between(9 * dz + d)
            near = [
                levels[dz][SLOTS * c : SLOTS * (c + 1), 128 * d : 128 * d + 128].reshape(4, 8, 128)
                for c in range(8)
            ]
            rx = own[0] - near[0]
            ry = own[1] - near[1]
            rz = own_z - near[2]
            dist_sq = rx * rx + ry * ry + rz * rz
            dist = dist_sq * lax.rsqrt(jnp.maximum(dist_sq, 1e-30))
            support = jnp.maximum(1.0 - dist, 0.0)
            cube = support * support * support
            approach = (own[4] - near[4]) * rx + (own[5] - near[5]) * ry + (own[6] - near[6]) * rz
            inverse = pl.reciprocal((dist_sq + visc_floor) * (own[7] + near[7]), approx=True)
            force = ((own[3] + near[3]) - jnp.minimum(approach, 0.0) * inverse) * cube
            for t, term in enumerate((force * rx, force * ry, force * rz, cube * approach)):
                total[t] = total[t] + jnp.sum(term, axis=0)
    sums = [jnp.sum(t, axis=0, keepdims=True) for t in total]
    row = lax.broadcasted_iota(jnp.int32, (8, 128), 0)
    rates = jnp.where(
        row < 2,
        jnp.where(row < 1, sums[0], sums[1]),
        jnp.where(row < 3, sums[2], sums[3]),
    )
    scale = -particle_mass * grad_scale
    return rates * jnp.where(row < 3, scale, -scale) - jnp.where(row == 2, gravity, 0.0)


def rates_kernel(later, *refs):
    columns_ref = refs[0]
    later_ref = refs[1] if later else None
    here_ref, select_ref, out_ref, *scratch = refs[1 + later :]
    parts_refs, spread_refs = scratch[:2], scratch[2:]
    step = pl.program_id(0)
    count = columns_ref.shape[2]

    def prepare(level, parts_ref):
        at = jnp.clip(level, 0, count - 1)

        def rows(ref):
            return jnp.concatenate(
                [ref[x, y, pl.ds(at, 1), :] for x in range(4) for y in range(4)], axis=0
            )

        inside = jnp.where((level >= 0) & (level < count), 1.0, 0.0)
        valid = here_ref[...] * inside > 0.5
        raw = jnp.where(valid, rows(columns_ref), 0.0)
        low, high = raw[:, :128], raw[:, 128:]
        if later:
            lane = lax.broadcasted_iota(jnp.int32, (16, 128), 1)
            low = low + 0.5 * time_step * jnp.where(lane < 96, high, 0.0)
            high = jnp.where(valid[:, :128], rows(later_ref), 0.0)
        parts_ref[...] = column_parts(low, high)

    def fill(n, parts_ref, target):
        tile = slice(256 * n, min(256 * n + 256, 9 * 128))
        target[:, tile] = jnp.dot(
            parts_ref[...], select_ref[:, tile], preferred_element_type=jnp.float32
        )

    @pl.when(step == 0)
    def _():
        for n in range(3):
            prepare(jnp.int32(n - 1), parts_refs[0])
            for tile in range(5):
                fill(tile, parts_refs[0], spread_refs[n])

    lane = lax.broadcasted_iota(jnp.int32, (SLOTS, 128), 1)
    slot = lax.broadcasted_iota(jnp.int32, (SLOTS, 128), 0)
    slot_mask = lane % SLOTS == slot
    for n in range(4):

        def between(place):
            if place == 0:
                prepare(step * 4 + n + 2, parts_refs[n % 2])
            elif place % 5 == 4:
                fill(place // 5, parts_refs[n % 2], spread_refs[(n + 3) % 4])

        out_ref[n] = pair_level([spread_refs[(n + i) % 4] for i in range(3)], slot_mask, between)


def rates_call(columns, here, later=None):
    levels = columns.shape[2]
    select = jnp.asarray(selector(), jnp.bfloat16)
    arrays = [columns] + ([] if later is None else [later])
    return pl.pallas_call(
        functools.partial(rates_kernel, later is not None),
        grid=(levels // 4,),
        out_shape=jax.ShapeDtypeStruct((levels, 8, 128), jnp.float32),
        in_specs=[pl.BlockSpec(a.shape, lambda k: (0, 0, 0, 0)) for a in arrays]
        + [
            pl.BlockSpec(here.shape, lambda k: (0, 0)),
            pl.BlockSpec(select.shape, lambda k: (0, 0)),
        ],
        out_specs=pl.BlockSpec((4, 8, 128), lambda k: (k, 0, 0)),
        scratch_shapes=[pltpu.VMEM((8 * SLOTS, 48), jnp.bfloat16) for _ in range(2)]
        + [pltpu.VMEM((8 * SLOTS, 9 * 128), jnp.float32) for _ in range(4)],
        compiler_params=pltpu.CompilerParams(vmem_limit_bytes=40 * 1024 * 1024),
    )(*arrays, here, select)


def by_column(rates):
    levels = rates.shape[0]
    return jnp.transpose(rates.reshape(levels, 8, 2, 2, SLOTS)[:, 0:4], (2, 3, 0, 1, 4))


def existing():
    slab, tile = lax.axis_index("slab"), lax.axis_index("tile")
    column = lax.broadcasted_iota(jnp.int32, (16, 256), 0)
    at_x = 2 * slab - 1 + column // 4
    at_y = 2 * tile - 1 + column % 4
    inside = (at_x >= 0) & (at_x < 2 * lax.axis_size("slab"))
    inside = inside & (at_y >= 0) & (at_y < 2 * lax.axis_size("tile"))
    return inside.astype(jnp.float32)


def pack_leavers(face_state, face_count, face_leave):
    cell_total = face_count.shape[0] * face_count.shape[1]
    row_total = cell_total * LMAX // 2
    leave_quota = face_leave.reshape(cell_total)
    occupancy = face_count.reshape(cell_total)
    row_ends = jnp.cumsum(leave_quota, dtype=jnp.int32)
    starts = row_ends - leave_quota
    row_ids = jnp.arange(row_total, dtype=jnp.int32)
    owner_mask = (starts[None, :] <= row_ids[:, None]) & (row_ends[None, :] > row_ids[:, None])
    root = jnp.arange(cell_total, dtype=jnp.int32) * SLOTS + occupancy - leave_quota - starts
    source_row = jnp.sum(jnp.where(owner_mask, root[None, :], 0), axis=1, dtype=jnp.int32) + row_ids
    flat_face = face_state.reshape(7, cell_total * SLOTS)
    return jnp.take(flat_face, source_row, axis=1)


def shards(particles, counts, leavers):
    levels = counts.shape[2]
    occ = occupied(counts)
    clean = jnp.where(occ[None], particles, 0.0)
    fields = jnp.concatenate([clean[0:3], occ.astype(jnp.float32)[None], clean[3:7]], axis=0)
    own = jnp.transpose(fields.reshape(8, 2, 2, levels, SLOTS), (1, 2, 3, 0, 4))
    here = existing()
    half = 0.5 * time_step
    columns = exchange(own.reshape(2, 2, levels, 8 * SLOTS), 0)
    rates_now = by_column(rates_call(columns, here))
    moved = jnp.where(own[..., 3:4, :] > 0.5, own[..., 4:8, :] + half * rates_now, 0.0)
    later = exchange(moved.reshape(2, 2, levels, 4 * SLOTS), 1)
    rates_mid = by_column(rates_call(columns, here, later))
    speed = own[..., 4:8, :] + time_step * rates_mid
    place = own[..., 0:3, :] + half * (own[..., 4:7, :] + speed[..., 0:3, :])
    updated = jnp.concatenate([place, speed], axis=3)
    updated = jnp.transpose(updated, (3, 0, 1, 2, 4)).reshape(7, 2, 2, levels * SLOTS)
    remain = counts.at[0].add(-leavers[0, 0]).at[1].add(-leavers[1, 0])
    kept = jnp.where(occupied(remain)[None], updated, 0.0)
    rows = jnp.stack([pack_leavers(updated[:, f], counts[f], leavers[f, 0]) for f in range(2)])
    return (kept, migrate(rows, 2))


def solution(mesh):
    return jax.shard_map(
        shards,
        mesh=mesh,
        in_specs=(
            P(None, "slab", "tile", None),
            P("slab", "tile", None),
            P(None, "slab", "tile", None),
        ),
        out_specs=(P(None, "slab", "tile", None), P(None, None, ("slab", "tile"))),
        check_vma=False,
    )
```
